128 devices in a mesh: lat: 8 (over z_lo, y), lon: 16 (over z_hi, x, core).
Axes of the slice: x: 4, y: 4, z: 4 (z_hi: 2, z_lo: 2; z = z_hi * 2 + z_lo), core: 2. Of those that a mesh axis runs over, the one named last changes fastest.
Arguments:
- latent: bfloat16 [2, 144, 384, 1024], P(None, 'lat', 'lon'), may hold values from -6 to 6
- grad_latent: bfloat16 [2, 144, 384, 1024], P(None, 'lat', 'lon'), may hold values from -6 to 6
- qkv_weight: bfloat16 [1024, 3072], replicated, may hold values from -0.1875 to 0.1875
- out_weight: bfloat16 [1024, 1024], replicated, may hold values from -0.1875 to 0.1875
- norm_gain: float32 [1024], replicated, may hold values from 0.25 to 1.75
- pair_bias: bfloat16 [16, 20736], replicated, may hold values from -4 to 390, as said below
Outputs:
- updated: bfloat16 [2, 144, 384, 1024], P(None, 'lat', 'lon')
- grad_input: bfloat16 [2, 144, 384, 1024], P(None, 'lat', 'lon')
- qkv_grad: float32 [1024, 3072], P(('lat', 'lon'))
- out_grad: float32 [1024, 1024], P(('lat', 'lon'))
The draws below stay inside these ranges and needn't reach their ends.
Inputs may be any that keep to these rules, and one draw needn't show every extreme that they name: pair_bias[h, 144 a + b] is the bias of head h for query token a and key token b of a window.
All inputs are finite; a program needn't handle non-finite values.
Results may differ from the reference program's by a relative error of at most 0.013.
Values may be sent and summed in bfloat16 or wider, within the bound.
No kernel may reach another device: no remote copies, remote signals or barrier semaphores. Data moves between devices by JAX's collectives and lax.ppermute only.
A program may use at most 256 MiB of HBM per device.

```python
import jax
import jax.numpy as jnp
from jax import lax

D = 1024
HEADS = 16
LEV = 2
WIN = 144
NLAT = 144
NLON = 384


def draw_pair_bias(key, part):
    key = jax.random.fold_in(key, 7)
    base_key = jax.random.fold_in(key, 0)
    table_len = WIN * WIN
    table = jnp.clip(jax.random.normal(base_key, (HEADS, table_len), jnp.float32), -4.0, 4.0)
    return table.astype(jnp.bfloat16)


def with_spikes(array, rng, source, target, blocks, factor):
    def block_of(dim):
        return (jnp.arange(array.shape[dim]) // (array.shape[dim] // blocks)).reshape((-1,) + (1,) * (array.ndim - 1 - dim))

    first = jax.random.permutation(rng, blocks)[block_of(target)]
    other_side = (block_of(target) + blocks // 2) % blocks
    return jnp.where((block_of(source) == first) | (block_of(source) == other_side), factor * array, array)


def steps_of(own_key, dims, cuts, smallest, top_value):
    def one(dim, parts):
        heights = jax.random.uniform(jax.random.fold_in(jax.random.fold_in(own_key, 6), dim), (parts,), jnp.float32, smallest / len(cuts), top_value / len(cuts))
        return jnp.repeat(jnp.exp(heights), dims[dim] // parts).reshape((-1,) + (1,) * (len(dims) - dim - 1))

    gain = one(*cuts[0])
    for cut in cuts[1:]:
        gain = gain * one(*cut)
    return gain


def normal_values(key, shape, deviation, bound, cuts=(), held_as=jnp.bfloat16):
    loudness = steps_of(key, shape, cuts, -0.22, 0.18) if cuts else 1.0
    values = jax.random.normal(key, shape, jnp.float32) * deviation * loudness
    return jnp.minimum(jnp.maximum(values, -bound), bound).astype(held_as)


def heavy_noise(key, shape, width, limit, shards, heavy, held_as=jnp.bfloat16):
    array = width * jax.random.normal(key, shape, jnp.float32)
    if shards:
        array = array * steps_of(key, shape, shards, -0.22, 0.18)
    return jnp.clip(with_spikes(array, jax.random.fold_in(key, 3), *heavy), -limit, limit).astype(held_as)


def setup_inputs(seed: int = 0) -> dict:
    seeds = jax.random.split(jax.random.key(seed), 7)
    latent = heavy_noise(seeds[0], (LEV, NLAT, NLON, D), 1.0, 6.0, ((1, 8), (2, 16)), (2, 3, 16, 2.0))
    grad_latent = normal_values(seeds[1], (LEV, NLAT, NLON, D), 1.0, 6.0, ((1, 8), (2, 16)))
    qkv_weight = normal_values(seeds[2], (D, 3 * D), D ** -0.5, 0.1875)
    out_weight = normal_values(seeds[3], (D, D), D ** -0.5, 0.1875)
    norm_gain = jnp.clip(1.0 + 0.15 * jax.random.normal(seeds[4], (D,), jnp.float32), 0.25, 1.75)
    pair_bias = draw_pair_bias(jax.random.fold_in(seeds[6], 71), 0)
    return dict(latent=latent, grad_latent=grad_latent, qkv_weight=qkv_weight, out_weight=out_weight, norm_gain=norm_gain, pair_bias=pair_bias)


def to_windows(tile):
    levels, tile_rows, tile_cols, features = tile.shape
    split = tile.reshape(levels, tile_rows // 6, 6, tile_cols // 12, 12, features)
    return split.transpose(1, 3, 0, 2, 4, 5).reshape(-1, levels * 72, features)

def from_windows(flat, levels, tile_rows, tile_cols):
    features = flat.shape[-1]
    split = flat.reshape(tile_rows // 6, tile_cols // 12, levels, 6, 12, features)
    return split.transpose(2, 0, 3, 1, 4, 5).reshape(levels, tile_rows, tile_cols, features)

def block_pass(x_tile, g_tile, pole_rows, norm_gain, qkv_weight, out_weight, pair_bias):
    levels, tile_rows, tile_cols, features = x_tile.shape
    head_count = pair_bias.shape[0]
    head_size = features // head_count
    window_len = levels * 72
    score_scale = head_size ** (-0.5)
    token_win = to_windows(x_tile)
    grad_win = to_windows(g_tile)
    window_count = token_win.shape[0]
    f32 = jnp.float32
    bf16 = jnp.bfloat16
    as_float = token_win.astype(f32)
    average = lax.optimization_barrier(jnp.mean(as_float, -1, keepdims=True))
    centred = as_float - average
    inv_std = lax.rsqrt(lax.optimization_barrier(jnp.mean(centred * centred, -1, keepdims=True)) + 1e-05)
    standard = centred * inv_std
    normed = (standard * norm_gain.astype(f32)).astype(bf16).reshape(-1, features)
    projected = jnp.dot(normed, qkv_weight, preferred_element_type=f32).astype(bf16)
    projected = projected.reshape(window_count, window_len, 3, head_count, head_size)
    query_part = projected[:, :, 0].astype(f32)
    key_part = projected[:, :, 1].astype(f32)
    value_part = projected[:, :, 2].astype(f32)
    upper_half = jnp.arange(window_len) % 72 // 12 >= 3
    differ = upper_half[:, None] != upper_half[None, :]
    pole_win = jnp.repeat(pole_rows, tile_cols // 12)
    blocked = pole_win[:, None, None, None] & differ[None, None]
    pair_table = pair_bias.astype(f32).reshape(head_count, window_len, window_len)
    scores = jnp.einsum('wqhd,wkhd->whqk', query_part, key_part) * score_scale + pair_table[None]
    scores = jnp.where(blocked, -1000000000.0, scores)
    peak_score = lax.optimization_barrier(jnp.max(scores, -1, keepdims=True))
    exponent = jnp.exp(scores - peak_score)
    soft = exponent / lax.optimization_barrier(jnp.sum(exponent, -1, keepdims=True))
    soft_b = soft.astype(bf16)
    attended = jnp.einsum('whqk,wkhd->wqhd', soft_b.astype(f32), value_part).astype(bf16).reshape(-1, features)
    result = (as_float.reshape(-1, features) + jnp.dot(attended, out_weight, preferred_element_type=f32)).astype(bf16)
    cotangent = grad_win.reshape(-1, features)
    term_output = jnp.einsum('ta,tb->ab', attended.astype(f32), cotangent.astype(f32))
    grad_attended = jnp.einsum('tb,ab->ta', cotangent.astype(f32), out_weight.astype(f32)).astype(bf16)
    grad_attended = grad_attended.reshape(window_count, window_len, head_count, head_size).astype(f32)
    grad_soft = jnp.einsum('wqhd,wkhd->whqk', grad_attended, value_part)
    inner_sum = lax.optimization_barrier(jnp.sum(soft * grad_soft, -1, keepdims=True))
    grad_scores = (soft * (grad_soft - inner_sum) * score_scale).astype(bf16).astype(f32)
    grad_query = jnp.einsum('whqk,wkhd->wqhd', grad_scores, key_part).astype(bf16)
    grad_key = jnp.einsum('whqk,wqhd->wkhd', grad_scores, query_part).astype(bf16)
    grad_value = jnp.einsum('whqk,wqhd->wkhd', soft_b.astype(f32), grad_attended).astype(bf16)
    grad_projected = jnp.stack([grad_query, grad_key, grad_value], 2).reshape(-1, 3 * features)
    term_proj = jnp.einsum('ta,tb->ab', normed.astype(f32), grad_projected.astype(f32))
    grad_normed = jnp.einsum('tb,ab->ta', grad_projected.astype(f32), qkv_weight.astype(f32))
    spread = grad_normed.reshape(window_count, window_len, features) * norm_gain.astype(f32)
    grad_branch = inv_std * (spread - lax.optimization_barrier(jnp.mean(spread, -1, keepdims=True)) - standard * lax.optimization_barrier(jnp.mean(spread * standard, -1, keepdims=True)))
    grad_total = (cotangent.astype(f32).reshape(window_count, window_len, features) + grad_branch).astype(bf16)
    out_tile = from_windows(result.reshape(window_count, window_len, features), levels, tile_rows, tile_cols)
    grad_tile = from_windows(grad_total, levels, tile_rows, tile_cols)
    return (out_tile, grad_tile, term_proj, term_output)

def reference(latent, grad_latent, qkv_weight, out_weight, norm_gain, pair_bias):
    levels, lat_cells, lon_cells, features = latent.shape
    rolled = jnp.roll(latent, (-3, -6), axis=(1, 2))
    rolled_grad = jnp.roll(grad_latent, (-3, -6), axis=(1, 2))
    blocks = lat_cells // 6
    token_blocks = rolled.reshape(levels, blocks, 6, lon_cells, features).transpose(1, 0, 2, 3, 4)
    grad_blocks = rolled_grad.reshape(levels, blocks, 6, lon_cells, features).transpose(1, 0, 2, 3, 4)

    def scan_step(running, sliced):
        token_tile, grad_tile, block_index = sliced
        pole_rows = (block_index == blocks - 1).reshape(1)
        out_tile, back_tile, term_proj, term_output = block_pass(token_tile, grad_tile, pole_rows, norm_gain, qkv_weight, out_weight, pair_bias)
        return ((running[0] + term_proj, running[1] + term_output), (out_tile, back_tile))
    zero_sums = (jnp.zeros((features, 3 * features), jnp.float32), jnp.zeros((features, features), jnp.float32))
    (sum_proj, sum_output), (out_blocks, back_blocks) = lax.scan(scan_step, zero_sums, (token_blocks, grad_blocks, jnp.arange(blocks, dtype=jnp.int32)))
    updated = out_blocks.transpose(1, 0, 2, 3, 4).reshape(levels, lat_cells, lon_cells, features)
    grad_input = back_blocks.transpose(1, 0, 2, 3, 4).reshape(levels, lat_cells, lon_cells, features)
    updated = jnp.roll(updated, (3, 6), axis=(1, 2))
    grad_input = jnp.roll(grad_input, (3, 6), axis=(1, 2))
    factor = float(levels * lat_cells * lon_cells) ** (-0.5)
    return (updated, grad_input, sum_proj * factor, sum_output * factor)
```

```python
import jax
import jax.numpy as jnp
from jax import lax
from jax.experimental import pallas as pl
from jax.experimental.pallas import tpu as pltpu
from jax.sharding import PartitionSpec as P

f32 = jnp.float32
bf16 = jnp.bfloat16
D = 1024
HEADS = 16
QUADS = 4
QW = 256
WIN = 144
TOK = 864
LANES = 4 * WIN
BLOCKED = -1e9
VMEM_LIMIT = 56 * 1024 * 1024
EPS = 1e-05


def nt(a, b):
    return lax.dot_general(a, b, (((1,), (1,)), ((), ())), preferred_element_type=f32)


def tn(a, b):
    return lax.dot_general(a, b, (((0,), (0,)), ((), ())), preferred_element_type=f32)


def nn(a, b):
    return jnp.dot(a, b, preferred_element_type=f32)


def index_of(x, y, z, c):
    return ((z % 2) * 4 + y) * 16 + (z // 2) * 8 + x * 2 + c


def place_of(index):
    lat, lon = index // 16, index % 16
    return dict(x=(lon // 2) % 4, y=lat % 4, z=(lon // 8) * 2 + lat // 4, c=lon % 2)


def my_place(axis):
    lat, lon = lax.axis_index("lat"), lax.axis_index("lon")
    return dict(x=(lon // 2) % 4, y=lat % 4, z=(lon // 8) * 2 + lat // 4, c=lon % 2)[axis]


def shift(value, axis, by):
    size = 2 if axis == "c" else 4
    pairs = []
    for src in range(128):
        place = place_of(src)
        place[axis] = (place[axis] + by) % size
        pairs.append((src, index_of(**place)))
    return lax.ppermute(value, ("lat", "lon"), pairs)


def shift_grid(value, dlat, dlon):
    pairs = []
    for lat in range(8):
        for lon in range(16):
            pairs.append((lat * 16 + lon, ((lat + dlat) % 8) * 16 + (lon + dlon) % 16))
    return lax.ppermute(value, ("lat", "lon"), pairs)


def row_order(axes):
    order = []
    for c in range(2):
        for i in range(4):
            for j in range(4):
                for k in range(4):
                    place = dict(zip(axes, (i, j, k)))
                    order.append(index_of(c=c, **place))
    return order


def ordered_rows(value, order):
    return jnp.concatenate([value[8 * p : 8 * p + 8] for p in order], 0)


def prologue_kernel(lat_ref, grad_ref, cols_ref, rows_ref, corner_ref, gain_ref, xw_ref, gw_ref, nt_ref, n_ref, xs, gs):
    for which, (tile, store) in enumerate(((lat_ref, xs), (grad_ref, gs))):
        for l in range(2):
            for i in range(18):
                if i < 15:
                    main = tile[l, i + 3].astype(f32)
                    side = cols_ref[which, l, i + 3].astype(f32)
                else:
                    main = rows_ref[which, l, i - 15].astype(f32)
                    side = corner_ref[which, l, i - 15].astype(f32)
                left = (i // 6) * 2 * WIN + l * 72 + (i % 6) * 12
                right = left + WIN
                store[left : left + 12] = main[6:18]
                store[right : right + 6] = main[18:24]
                store[right + 6 : right + 12] = side
    order = row_order("xyz")
    gain = gain_ref[...]

    for w in range(6):
        rows = pl.ds(w * WIN, WIN)
        x = xs[rows]
        centred = x - jnp.mean(x, -1, keepdims=True)
        inv_std = lax.rsqrt(jnp.mean(centred * centred, -1, keepdims=True) + EPS)
        normed = centred * inv_std * gain
        n_ref[rows] = normed.astype(bf16)
        xw_ref[rows] = x.astype(bf16)
        gw_ref[rows] = gs[rows].astype(bf16)
    for half in range(4):
        block = n_ref[:, half * QW : (half + 1) * QW].astype(f32)
        nt_ref[half * QW : (half + 1) * QW] = block.T.astype(bf16)


def prologue(latent, grad_latent, cols, rows, corner, gain):
    return pl.pallas_call(
        prologue_kernel,
        out_shape=(
            jax.ShapeDtypeStruct((TOK, D), bf16),
            jax.ShapeDtypeStruct((TOK, D), bf16),
            jax.ShapeDtypeStruct((D, TOK), bf16),
            jax.ShapeDtypeStruct((TOK, D), bf16),
        ),
        scratch_shapes=[pltpu.VMEM((TOK, D), f32), pltpu.VMEM((TOK, D), f32)],
        compiler_params=pltpu.CompilerParams(vmem_limit_bytes=VMEM_LIMIT),
        name="prologue",
    )(latent, grad_latent, cols, rows, corner, gain)


def quad_kernel(
    pole_ref, n_ref, nt_ref, gw_ref, wq_ref, wk_ref, wv_ref, wo_ref, bias_ref,
    att_ref, gp_ref, grad_ref, q, k, v, da,
):
    n = n_ref[...]
    q[...] = nn(n, wq_ref[...]).astype(bf16)
    k[...] = nn(n, wk_ref[...]).astype(bf16)
    v[...] = nn(n, wv_ref[...]).astype(bf16)
    da[...] = nt(gw_ref[...], wo_ref[...]).astype(bf16)
    lane_head = lax.broadcasted_iota(jnp.int32, (WIN, QW), 1) // 64

    def apart(value):
        zero = jnp.zeros_like(value)
        return jnp.concatenate([jnp.where(lane_head == h, value, zero) for h in range(4)], 0)

    def gathered(stacked):
        out = stacked[:WIN]
        for h in range(1, 4):
            out = jnp.where(lane_head == h, stacked[h * WIN : (h + 1) * WIN], out)
        return out

    def window(w, carry):
        rows = pl.ds(pl.multiple_of(w * WIN, WIN), WIN)
        variant = jnp.where(w >= 4, pole_ref[0], 0)
        qw, kw, vw, dw = q[rows], k[rows], v[rows], da[rows]
        q_apart = apart(qw * jnp.asarray(0.125, bf16))
        d_apart = apart(dw)
        s = nt(kw, q_apart) + bias_ref[variant, 0].astype(f32)
        e = jnp.exp(s - jnp.max(s, 0, keepdims=True))
        soft = e * (1.0 / jnp.sum(e, 0, keepdims=True))
        soft_b = soft.astype(bf16)
        att_ref[rows] = gathered(tn(soft_b, vw)).astype(bf16)
        dv = nn(soft_b, d_apart)
        dp = nt(vw, d_apart)
        inner = jnp.sum(soft * dp, 0, keepdims=True)
        ds = (soft * (dp - inner)).astype(bf16)
        dk = nn(ds, q_apart)
        dq = gathered(tn(ds, kw)) * 0.125
        gp_ref[0, rows] = dq.astype(bf16)
        gp_ref[1, rows] = dk.astype(bf16)
        gp_ref[2, rows] = dv.astype(bf16)
        return carry

    lax.fori_loop(0, 6, window, 0)
    order = row_order("xyz")
    for part in range(3):
        grad_ref[:, part] = ordered_rows(nn(nt_ref[...], gp_ref[part]), order).astype(bf16).reshape(2, 512, QW)


def quads(pole, normed, normed_t, gw, qkv_weight, out_weight, bias, first, count):
    def whole(shape):
        return pl.BlockSpec(shape, lambda g, pole: (0,) * len(shape))

    def columns(part):
        return pl.BlockSpec((D, QW), lambda g, pole: (0, part * QUADS + first + g))

    return pl.pallas_call(
        quad_kernel,
        grid_spec=pltpu.PrefetchScalarGridSpec(
            num_scalar_prefetch=1,
            grid=(count,),
            in_specs=[
                whole((TOK, D)), whole((D, TOK)), whole((TOK, D)),
                columns(0), columns(1), columns(2),
                pl.BlockSpec((QW, D), lambda g, pole: (first + g, 0)),
                pl.BlockSpec((2, 1, WIN, LANES), lambda g, pole: (0, first + g, 0, 0)),
            ],
            out_specs=[
                pl.BlockSpec((TOK, QW), lambda g, pole: (0, g)),
                pl.BlockSpec((3, TOK, QW), lambda g, pole: (0, 0, g)),
                pl.BlockSpec((2, 3, 512, QW), lambda g, pole: (0, 0, 0, g)),
            ],
            scratch_shapes=[pltpu.VMEM((TOK, QW), bf16)] * 4,
        ),
        out_shape=(
            jax.ShapeDtypeStruct((TOK, count * QW), bf16),
            jax.ShapeDtypeStruct((3, TOK, count * QW), bf16),
            jax.ShapeDtypeStruct((2, 3, 512, count * QW), bf16),
        ),
        compiler_params=pltpu.CompilerParams(vmem_limit_bytes=VMEM_LIMIT),
        name="quads",
    )(pole, normed, normed_t, gw, qkv_weight, qkv_weight, qkv_weight, out_weight, bias)


def out_grad_kernel(att_ref, gw_ref, grad_ref):
    order = row_order("xyz")
    att = att_ref[...].astype(f32).T.astype(bf16)
    grad_ref[...] = ordered_rows(nn(att, gw_ref[...]), order).astype(bf16).reshape(2, 512, QW)


def out_grads(att, gw):
    return pl.pallas_call(
        out_grad_kernel,
        grid=(QUADS,),
        in_specs=[pl.BlockSpec((TOK, D), lambda n: (0, 0)), pl.BlockSpec((TOK, QW), lambda n: (0, n))],
        out_specs=pl.BlockSpec((2, 512, QW), lambda n: (0, 0, n)),
        out_shape=jax.ShapeDtypeStruct((2, 512, D), bf16),
        compiler_params=pltpu.CompilerParams(vmem_limit_bytes=VMEM_LIMIT),
        name="out_grads",
    )(att, gw)


def epilogue_kernel(att_ref, gp_ref, wo_ref, w_ref, xw_ref, gw_ref, gain_ref, out_ref, grad_ref, so, sg):
    x = xw_ref[...].astype(f32)
    so[...] = x + nn(att_ref[...], wo_ref[...])
    gn = nt(gp_ref[0], w_ref[:, :D]) + nt(gp_ref[1], w_ref[:, D : 2 * D]) + nt(gp_ref[2], w_ref[:, 2 * D :])
    centred = x - jnp.mean(x, -1, keepdims=True)
    inv_std = lax.rsqrt(jnp.mean(centred * centred, -1, keepdims=True) + EPS)
    unit = centred * inv_std
    e = gn * gain_ref[...]
    branch = inv_std * (e - jnp.mean(e, -1, keepdims=True) - unit * jnp.mean(e * unit, -1, keepdims=True))
    sg[...] = gw_ref[...].astype(f32) + branch
    for l in range(2):
        for r in range(6):
            at = l * 72 + r * 12
            for src, dst in ((so, out_ref), (sg, grad_ref)):
                line = jnp.concatenate([src[at : at + 12], src[WIN + at : WIN + at + 12]], 0)
                dst[l, r] = line.astype(bf16)


def epilogue(att, gp, out_weight, qkv_weight, xw, gw, gain):
    rows = 2 * WIN
    tile = pl.BlockSpec((2, 6, 24, D), lambda i: (0, i, 0, 0))
    return pl.pallas_call(
        epilogue_kernel,
        grid=(3,),
        in_specs=[
            pl.BlockSpec((rows, D), lambda i: (i, 0)),
            pl.BlockSpec((3, rows, D), lambda i: (0, i, 0)),
            pl.BlockSpec((D, D), lambda i: (0, 0)),
            pl.BlockSpec((D, 3 * D), lambda i: (0, 0)),
            pl.BlockSpec((rows, D), lambda i: (i, 0)),
            pl.BlockSpec((rows, D), lambda i: (i, 0)),
            pl.BlockSpec((1, D), lambda i: (0, 0)),
        ],
        out_specs=[tile, tile],
        out_shape=[jax.ShapeDtypeStruct((2, 18, 24, D), bf16)] * 2,
        scratch_shapes=[pltpu.VMEM((rows, D), f32)] * 2,
        compiler_params=pltpu.CompilerParams(vmem_limit_bytes=VMEM_LIMIT),
        name="epilogue",
    )(att, gp, out_weight, qkv_weight, xw, gw, gain)


def restore_kernel(out_ref, grad_ref, cols_ref, rows_ref, corner_ref, updated_ref, back_ref):
    for which, (src, dst) in enumerate(((out_ref, updated_ref), (grad_ref, back_ref))):
        for l in range(2):
            for i in range(18):
                if i < 3:
                    main = rows_ref[which, l, i].astype(f32)
                    side = corner_ref[which, l, i].astype(f32)
                else:
                    main = src[l, i - 3].astype(f32)
                    side = cols_ref[which, l, i - 3].astype(f32)
                dst[l, i] = jnp.concatenate([side, main[:18]], 0).astype(bf16)


def restored(out, grad, cols, rows, corner):
    return pl.pallas_call(
        restore_kernel,
        out_shape=[jax.ShapeDtypeStruct((2, 18, 24, D), bf16)] * 2,
        compiler_params=pltpu.CompilerParams(vmem_limit_bytes=VMEM_LIMIT),
        name="restore",
    )(out, grad, cols, rows, corner)


def pick(v, i):
    return lax.dynamic_index_in_dim(v, i, 0, keepdims=False)


def core_stage(v):
    m = my_place("c")
    r = shift(pick(v, 1 - m), "c", 1)
    return (pick(v, m).astype(f32) + r.astype(f32)).astype(bf16)


def ring_stage(v, axis):
    m = my_place(axis)
    up = shift(pick(v, (m + 1) % 4), axis, 1)
    down = shift(pick(v, (m + 3) % 4), axis, -1)
    far = shift(pick(v, (m + 2) % 4), axis, 2)
    return pick(v, m).astype(f32) + up.astype(f32) + down.astype(f32) + far.astype(f32)


def reduce_scatter(v, order):
    v = core_stage(v)
    for i, axis in enumerate(order):
        v = ring_stage(v.reshape(4, -1, v.shape[-1]), axis)
        if i < 2:
            v = v.astype(bf16)
    return v


def per_device(latent, grad_latent, qkv_weight, out_weight, norm_gain, pair_bias):
    both = jnp.stack([latent, grad_latent])
    cols = shift_grid(both[:, :, :, :6], 0, -1)
    rows = shift_grid(both[:, :, :3], -1, 0)
    corner = shift_grid(both[:, :, :3, :6], -1, -1)
    gain = norm_gain.reshape(1, D)

    table = pair_bias.reshape(QUADS, 4, WIN, WIN).transpose(0, 3, 1, 2)
    upper = jnp.arange(WIN) % 72 // 12 >= 3
    differ = upper[:, None, None] != upper[None, None, :]
    bias = jnp.stack([table, jnp.where(differ, jnp.asarray(BLOCKED, bf16), table)])
    bias = bias.reshape(2, QUADS, WIN, LANES)
    pole = (lax.axis_index("lat") == lax.axis_size("lat") - 1).astype(jnp.int32).reshape(1)

    xw, gw, normed_t, normed = prologue(latent, grad_latent, cols, rows, corner, gain)
    att, gp, qkv_part = quads(pole, normed, normed_t, gw, qkv_weight, out_weight, bias, 0, QUADS)
    out_part = out_grads(att, gw)
    out_tile, grad_tile = epilogue(att, gp, out_weight, qkv_weight, xw, gw, gain)
    tiles = jnp.stack([out_tile, grad_tile])
    cols = shift_grid(tiles[:, :, :15, 18:], 0, 1)
    rows = shift_grid(tiles[:, :, 15:], 1, 0)
    corner = shift_grid(tiles[:, :, 15:, 18:], 1, 1)
    updated, grad_input = restored(out_tile, grad_tile, cols, rows, corner)

    factor = 110592.0 ** (-0.5)
    part = jnp.concatenate([qkv_part, out_part[:, None]], 1)
    part = part.transpose(0, 2, 1, 3).reshape(2, 512, 4 * D)
    grads = reduce_scatter(part, "xyz") * factor
    return (updated, grad_input, grads[:, : 3 * D], grads[:, 3 * D :])


def solution(mesh):
    in_specs = (P(None, "lat", "lon", None), P(None, "lat", "lon", None), P(), P(), P(), P())
    out_specs = (
        P(None, "lat", "lon", None),
        P(None, "lat", "lon", None),
        P(("lat", "lon"), None),
        P(("lat", "lon"), None),
    )
    return jax.shard_map(
        per_device, mesh=mesh, in_specs=in_specs, out_specs=out_specs, check_vma=False
    )
```

```python
import jax
import jax.numpy as jnp
from jax import lax
from jax.experimental import pallas as pl
from jax.experimental.pallas import tpu as pltpu
from jax.sharding import PartitionSpec as P

f32 = jnp.float32
bf16 = jnp.bfloat16
D = 1024
HEADS = 16
QUADS = 4
QW = 256
WIN = 144
TOK = 864
LANES = 4 * WIN
BLOCKED = -1e9
EPS = 1e-05


def nt(a, b):
    return lax.dot_general(a, b, (((1,), (1,)), ((), ())), preferred_element_type=f32)


def tn(a, b):
    return lax.dot_general(a, b, (((0,), (0,)), ((), ())), preferred_element_type=f32)


def nn(a, b):
    return jnp.dot(a, b, preferred_element_type=f32)


def index_of(x, y, z, c):
    return ((z % 2) * 4 + y) * 16 + (z // 2) * 8 + x * 2 + c


def place_of(index):
    lat, lon = index // 16, index % 16
    return dict(x=(lon // 2) % 4, y=lat % 4, z=(lon // 8) * 2 + lat // 4, c=lon % 2)


def my_place(axis):
    lat, lon = lax.axis_index("lat"), lax.axis_index("lon")
    return dict(x=(lon // 2) % 4, y=lat % 4, z=(lon // 8) * 2 + lat // 4, c=lon % 2)[axis]


def shift(value, axis, by):
    size = 2 if axis == "c" else 4
    pairs = []
    for src in range(128):
        place = place_of(src)
        place[axis] = (place[axis] + by) % size
        pairs.append((src, index_of(**place)))
    return lax.ppermute(value, ("lat", "lon"), pairs)


def shift_grid(value, dlat, dlon):
    pairs = []
    for lat in range(8):
        for lon in range(16):
            pairs.append((lat * 16 + lon, ((lat + dlat) % 8) * 16 + (lon + dlon) % 16))
    return lax.ppermute(value, ("lat", "lon"), pairs)


RINGS = ("xyz", "yxz")


def relative_rows():
    owner = place_of(jnp.arange(128, dtype=jnp.int32))
    off = {axis: (owner[axis] - my_place(axis)) % 4 for axis in "xyz"}
    along = [(off[a] * 4 + off[b]) * 4 + off[c] for a, b, c in RINGS]
    return (owner["c"] - my_place("c")) % 2 * 64 + jnp.where(owner["c"] == 0, along[0], along[1])


def ring_shift(value, stage, by):
    pairs = []
    for src in range(128):
        place = place_of(src)
        axis = RINGS[place["c"]][stage]
        place[axis] = (place[axis] + by) % 4
        pairs.append((src, index_of(**place)))
    return lax.ppermute(value, ("lat", "lon"), pairs)


def ring(pieces, stage):
    return [ring_shift(pieces[1], stage, 1), ring_shift(pieces[3], stage, -1), ring_shift(pieces[2], stage, 2)]


def params(mib):
    return pltpu.CompilerParams(vmem_limit_bytes=mib * 1024 * 1024)


def once(shape):
    return pl.BlockSpec(shape, lambda *_: (0,) * len(shape), pipeline_mode=pl.Buffered(1))


def cost(us):
    return pl.CostEstimate(flops=int(us * 1e9), bytes_accessed=int(us * 3e5), transcendentals=0)


def shaped(shape, dtype=bf16):
    return jax.ShapeDtypeStruct(shape, dtype)


VMEM = pl.BlockSpec(memory_space=pltpu.VMEM)
SMEM = pl.BlockSpec(memory_space=pltpu.SMEM)
COLS, ROWS, CORNER = 432, 288, 80


def strips_kernel(lat_ref, grad_ref, cols_ref, rows_ref, corner_ref, cs, rs, ks):
    ks[72:80] = jnp.zeros((8, D), f32)
    for which, tile in enumerate((lat_ref, grad_ref)):
        for l in range(2):
            for i in range(18):
                line = tile[l, i].astype(f32)
                at = (which * 2 + l) * 18 + i
                cs[at * 6 : at * 6 + 6] = line[:6]
                if i < 3:
                    at = (which * 2 + l) * 3 + i
                    rs[at * 24 : at * 24 + 24] = line
                    ks[at * 6 : at * 6 + 6] = line[:6]
    cols_ref[...] = cs[...].astype(bf16)
    rows_ref[...] = rs[...].astype(bf16)
    corner_ref[...] = ks[...].astype(bf16)


def strips(latent, grad_latent):
    return pl.pallas_call(
        strips_kernel,
        in_specs=[VMEM] * 2,
        out_specs=[VMEM] * 3,
        out_shape=[shaped((COLS, D)), shaped((ROWS, D)), shaped((CORNER, D))],
        scratch_shapes=[pltpu.VMEM((n, D), f32) for n in (COLS, ROWS, CORNER)],
        compiler_params=params(20),
        cost_estimate=cost(3),
        name="strips",
    )(latent, grad_latent)


def turned(value, place_ref, first, store):
    t = value.T
    for p in range(t.shape[0] // 8):
        store[pl.ds(pl.multiple_of(place_ref[first + p] * 8, 8), 8)] = t[8 * p : 8 * p + 8]


def prologue_kernel(
    place_ref, lat_ref, grad_ref, cols_ref, rows_ref, corner_ref, gain_ref, xw_ref, gw_ref, nt_ref, n_ref, xs, gs, ts, cs, ks
):
    cs[...] = cols_ref[...].astype(f32)
    ks[...] = corner_ref[...].astype(f32)
    for which, (tile, store) in enumerate(((lat_ref, xs), (grad_ref, gs))):
        for l in range(2):
            for i in range(18):
                if i < 15:
                    main = tile[l, i + 3].astype(f32)
                    at = ((which * 2 + l) * 18 + i + 3) * 6
                    side = cs[at : at + 6]
                else:
                    at = (which * 2 + l) * 3 + i - 15
                    main = rows_ref[at * 24 : at * 24 + 24].astype(f32)
                    side = ks[at * 6 : at * 6 + 6]
                left = (i // 6) * 2 * WIN + l * 72 + (i % 6) * 12
                right = left + WIN
                store[left : left + 12] = main[6:18]
                store[right : right + 6] = main[18:24]
                store[right + 6 : right + 12] = side
    gain = gain_ref[...]
    for w in range(6):
        rows = pl.ds(w * WIN, WIN)
        x = xs[rows]
        centred = x - jnp.mean(x, -1, keepdims=True)
        inv_std = lax.rsqrt(jnp.mean(centred * centred, -1, keepdims=True) + EPS)
        xw_ref[rows] = x.astype(bf16)
        gw_ref[rows] = gs[rows].astype(bf16)
        normed = centred * inv_std * gain
        n_ref[rows] = normed.astype(bf16)
        xs[rows] = normed
    for g in range(4):
        turned(xs[:, g * QW : (g + 1) * QW], place_ref, g * 32, ts)
    nt_ref[...] = ts[...].astype(bf16)


def prologue(place, latent, grad_latent, cols, rows, corner, gain):
    return pl.pallas_call(
        prologue_kernel,
        in_specs=[SMEM] + [VMEM] * 6,
        out_specs=[VMEM] * 4,
        out_shape=[shaped((TOK, D)), shaped((TOK, D)), shaped((D, TOK)), shaped((TOK, D))],
        scratch_shapes=[
            pltpu.VMEM((TOK, D), f32), pltpu.VMEM((TOK, D), f32), pltpu.VMEM((D, TOK), f32),
            pltpu.VMEM((COLS, D), f32), pltpu.VMEM((CORNER, D), f32),
        ],
        compiler_params=params(34),
        cost_estimate=cost(7),
        name="prologue",
    )(place, latent, grad_latent, cols, rows, corner, gain)


def attention(pole, n_ref, gw_ref, wq_ref, wk_ref, wv_ref, wo_ref, bias_ref, att_ref, gp_ref, q, k, v, da):
    n = n_ref[...]
    q[...] = nn(n, wq_ref[...]).astype(bf16)
    k[...] = nn(n, wk_ref[...]).astype(bf16)
    v[...] = nn(n, wv_ref[...]).astype(bf16)
    da[...] = nt(gw_ref[...], wo_ref[...]).astype(bf16)
    lane_head = lax.broadcasted_iota(jnp.int32, (WIN, QW), 1) // 64

    def apart(value):
        zero = jnp.zeros_like(value)
        return jnp.concatenate([jnp.where(lane_head == h, value, zero) for h in range(4)], 0)

    def gathered(stacked):
        out = stacked[:WIN]
        for h in range(1, 4):
            out = jnp.where(lane_head == h, stacked[h * WIN : (h + 1) * WIN], out)
        return out

    def window(w, carry):
        rows = pl.ds(pl.multiple_of(w * WIN, WIN), WIN)
        variant = jnp.where(w >= 4, pole, 0)
        qw, kw, vw, dw = q[rows], k[rows], v[rows], da[rows]
        q_apart = apart(qw * jnp.asarray(0.125, bf16))
        d_apart = apart(dw)
        s = nt(kw, q_apart) + bias_ref[variant, 0].astype(f32)
        e = jnp.exp(s - jnp.max(s, 0, keepdims=True))
        soft = e * (1.0 / jnp.sum(e, 0, keepdims=True))
        soft_b = soft.astype(bf16)
        att_ref[rows] = gathered(tn(soft_b, vw)).astype(bf16)
        dv = nn(soft_b, d_apart)
        dp = nt(vw, d_apart)
        inner = jnp.sum(soft * dp, 0, keepdims=True)
        ds = (soft * (dp - inner)).astype(bf16)
        dk = nn(ds, q_apart)
        dq = gathered(tn(ds, kw)) * 0.125
        gp_ref[0, rows] = dq.astype(bf16)
        gp_ref[1, rows] = dk.astype(bf16)
        gp_ref[2, rows] = dv.astype(bf16)
        return carry

    lax.fori_loop(0, 6, window, 0)


def split_rows(value, keep_ref, send_ref, at):
    keep_ref[:, at : at + QW] = value[:512].astype(bf16)
    send_ref[:, at : at + QW] = value[512:].astype(bf16)


def quads_kernel(
    pole_ref, n_ref, nt_ref, gw_ref, wq_ref, wk_ref, wv_ref, wo_ref, bias_ref,
    att_ref, gp_ref, keep_ref, send_ref, q, k, v, da,
):
    attention(pole_ref[0], n_ref, gw_ref, wq_ref, wk_ref, wv_ref, wo_ref, bias_ref, att_ref, gp_ref, q, k, v, da)
    for part in range(3):
        split_rows(nn(nt_ref[...], gp_ref[part]), keep_ref, send_ref, part * QW)


def out_grads_kernel(place_ref, before_ref, after_ref, gw_ref, keep_ref, send_ref, ts):
    for g in range(4):
        att = before_ref[:, g * QW : (g + 1) * QW] if g < 3 else after_ref[...]
        turned(att.astype(f32), place_ref, g * 32, ts)
    turned_att = ts[...].astype(bf16)
    for part in range(4):
        at = part * QW
        split_rows(nn(turned_att, gw_ref[:, at : at + QW]), keep_ref, send_ref, at)


FIRST = 3


def quad_specs(first):
    def columns(part):
        return pl.BlockSpec((D, QW), lambda g, *_: (0, part * QUADS + first + g))

    return [
        once((TOK, D)), once((D, TOK)), once((TOK, D)),
        columns(0), columns(1), columns(2),
        pl.BlockSpec((QW, D), lambda g, *_: (first + g, 0)),
        pl.BlockSpec((2, 1, WIN, LANES), lambda g, *_: (0, first + g, 0, 0)),
    ]


def some_quads(first, count, pole, normed, normed_t, gw, qkv_weight, out_weight, bias):
    return pl.pallas_call(
        quads_kernel,
        grid_spec=pltpu.PrefetchScalarGridSpec(
            num_scalar_prefetch=1,
            grid=(count,),
            in_specs=quad_specs(first),
            out_specs=[
                pl.BlockSpec((TOK, QW), lambda g, pole: (0, g)),
                pl.BlockSpec((3, TOK, QW), lambda g, pole: (0, 0, g)),
                pl.BlockSpec((512, 3 * QW), lambda g, pole: (0, g)),
                pl.BlockSpec((512, 3 * QW), lambda g, pole: (0, g)),
            ],
            scratch_shapes=[pltpu.VMEM((TOK, QW), bf16)] * 4,
        ),
        out_shape=[
            shaped((TOK, count * QW)), shaped((3, TOK, count * QW)),
            shaped((512, count * 3 * QW)), shaped((512, count * 3 * QW)),
        ],
        compiler_params=params(40),
        cost_estimate=cost(11 * count),
        name="quads",
    )(pole, normed, normed_t, gw, qkv_weight, qkv_weight, qkv_weight, out_weight, bias)


def out_grads(place, before, after, gw):
    return pl.pallas_call(
        out_grads_kernel,
        in_specs=[SMEM] + [VMEM] * 3,
        out_specs=[VMEM] * 2,
        out_shape=[shaped((512, D))] * 2,
        scratch_shapes=[pltpu.VMEM((D, TOK), f32)],
        compiler_params=params(20),
        cost_estimate=cost(7),
        name="out_grads",
    )(place, before, after, gw)


def epilogue_kernel(
    att_ref, att2_ref, gp_ref, gp2_ref, wo_ref, w_ref, xw_ref, gw_ref, gain_ref,
    out_ref, grad_ref, cols_ref, rows_ref, corner_ref, so, sg, cs, rs, ks,
):
    at_first = FIRST * QW
    x = xw_ref[...].astype(f32)
    so[...] = x + nn(att_ref[...], wo_ref[:at_first]) + nn(att2_ref[...], wo_ref[at_first:])
    gn = jnp.zeros((2 * WIN, D), f32)
    for part in range(3):
        gn = gn + nt(gp_ref[part], w_ref[:, part * D : part * D + at_first])
        gn = gn + nt(gp2_ref[part], w_ref[:, part * D + at_first : (part + 1) * D])
    centred = x - jnp.mean(x, -1, keepdims=True)
    inv_std = lax.rsqrt(jnp.mean(centred * centred, -1, keepdims=True) + EPS)
    unit = centred * inv_std
    e = gn * gain_ref[...]
    branch = inv_std * (e - jnp.mean(e, -1, keepdims=True) - unit * jnp.mean(e * unit, -1, keepdims=True))
    sg[...] = gw_ref[...].astype(f32) + branch
    step = pl.program_id(0)
    for which, (src, dst) in enumerate(((so, out_ref), (sg, grad_ref))):
        for l in range(2):
            for r in range(6):
                at = l * 72 + r * 12
                line = jnp.concatenate([src[at : at + 12], src[WIN + at : WIN + at + 12]], 0)
                dst[l, r] = line.astype(bf16)
                to = ((which * 2 + l) * 6 + r) * 6
                cs[to : to + 6] = line[18:]
                if r >= 3:
                    to = (which * 2 + l) * 3 + r - 3
                    rs[to * 24 : to * 24 + 24] = line
                    ks[to * 6 : to * 6 + 6] = line[18:]
    cols_ref[0] = cs[...].astype(bf16)

    @pl.when(step == 2)
    def _():
        ks[72:80] = jnp.zeros((8, D), f32)
        rows_ref[...] = rs[...].astype(bf16)
        corner_ref[...] = ks[...].astype(bf16)


def epilogue(att, att2, gp, gp2, out_weight, qkv_weight, xw, gw, gain):
    rows = 2 * WIN
    tile = pl.BlockSpec((2, 6, 24, D), lambda i: (0, i, 0, 0))
    return pl.pallas_call(
        epilogue_kernel,
        grid=(3,),
        in_specs=[
            pl.BlockSpec((rows, FIRST * QW), lambda i: (i, 0)),
            pl.BlockSpec((rows, QW), lambda i: (i, 0)),
            pl.BlockSpec((3, rows, FIRST * QW), lambda i: (0, i, 0)),
            pl.BlockSpec((3, rows, QW), lambda i: (0, i, 0)),
            once((D, D)),
            once((D, 3 * D)),
            pl.BlockSpec((rows, D), lambda i: (i, 0)),
            pl.BlockSpec((rows, D), lambda i: (i, 0)),
            pl.BlockSpec((1, D), lambda i: (0, 0)),
        ],
        out_specs=[
            tile, tile,
            pl.BlockSpec((1, WIN, D), lambda i: (i, 0, 0)),
            pl.BlockSpec((ROWS, D), lambda i: (0, 0)),
            pl.BlockSpec((CORNER, D), lambda i: (0, 0)),
        ],
        out_shape=[shaped((2, 18, 24, D))] * 2 + [shaped((3, WIN, D)), shaped((ROWS, D)), shaped((CORNER, D))],
        scratch_shapes=[pltpu.VMEM((n, D), f32) for n in (rows, rows, WIN, ROWS, CORNER)],
        compiler_params=params(40),
        cost_estimate=cost(16),
        name="epilogue",
    )(att, att2, gp, gp2, out_weight, qkv_weight, xw, gw, gain)


def restore_kernel(out_ref, grad_ref, cols_ref, rows_ref, corner_ref, updated_ref, back_ref, cs, ks):
    cs[...] = cols_ref[...].astype(f32)
    ks[...] = corner_ref[...].astype(f32)
    for which, (src, dst) in enumerate(((out_ref, updated_ref), (grad_ref, back_ref))):
        for l in range(2):
            for i in range(18):
                if i < 3:
                    at = (which * 2 + l) * 3 + i
                    main = rows_ref[at * 24 : at * 24 + 24].astype(f32)
                    side = ks[at * 6 : at * 6 + 6]
                else:
                    main = src[l, i - 3].astype(f32)
                    at = ((which * 2 + l) * 6 + (i - 3) % 6) * 6
                    side = cs[(i - 3) // 6, at : at + 6]
                dst[l, i] = jnp.concatenate([side, main[:18]], 0).astype(bf16)


def restored(out, grad, cols, rows, corner):
    return pl.pallas_call(
        restore_kernel,
        in_specs=[VMEM] * 5,
        out_specs=[VMEM] * 2,
        out_shape=[shaped((2, 18, 24, D))] * 2,
        scratch_shapes=[pltpu.VMEM((3, WIN, D), f32), pltpu.VMEM((CORNER, D), f32)],
        compiler_params=params(24),
        cost_estimate=cost(5),
        name="restore",
    )(out, grad, cols, rows, corner)


def core_sum_kernel(*refs):
    ins, outs = refs[:-4], refs[-4:]
    at = 0
    for keep, got in zip(ins[::2], ins[1::2]):
        columns = slice(at, at + keep.shape[1])
        for i, out in enumerate(outs):
            rows = slice(i * 128, i * 128 + 128)
            out[:, columns] = (keep[rows].astype(f32) + got[rows].astype(f32)).astype(bf16)
        at += keep.shape[1]


def core_sum(*pairs):
    columns = sum(v.shape[1] for v in pairs[::2])
    return pl.pallas_call(
        core_sum_kernel,
        in_specs=[VMEM] * len(pairs),
        out_specs=[VMEM] * 4,
        out_shape=[shaped((128, columns))] * 4,
        compiler_params=params(16),
        cost_estimate=cost(2),
        name="core_sum",
    )(*pairs)


def summed(refs):
    total = refs[0][...].astype(f32)
    for ref in refs[1:]:
        total = total + ref[...].astype(f32)
    return total


def ring_sum_kernel(*refs):
    ins, outs = refs[:-4], refs[-4:]
    at = 0
    for first in range(0, len(ins), 4):
        total = summed(ins[first : first + 4])
        rows = total.shape[0] // 4
        for i, out in enumerate(outs):
            out[:, at : at + total.shape[1]] = total[i * rows : (i + 1) * rows].astype(out.dtype)
        at += total.shape[1]


def ring_sum(dtype, *groups):
    rows = groups[0][0].shape[0] // 4
    columns = sum(group[0].shape[1] for group in groups)
    return pl.pallas_call(
        ring_sum_kernel,
        in_specs=[VMEM] * (4 * len(groups)),
        out_specs=[VMEM] * 4,
        out_shape=[shaped((rows, columns), dtype)] * 4,
        compiler_params=params(12),
        cost_estimate=cost(1),
        name="ring_sum",
    )(*[v for group in groups for v in group])


def finish_kernel(a, b, c, d, qkv_ref, out_ref):
    total = summed((a, b, c, d)) * (110592.0 ** (-0.5))
    for g in range(4):
        for part in range(3):
            at = (g * 3 + part) * QW
            to = part * D + g * QW
            qkv_ref[:, to : to + QW] = total[:, at : at + QW]
    out_ref[...] = total[:, 3 * D :]


def finish(own, got):
    return pl.pallas_call(
        finish_kernel,
        in_specs=[VMEM] * 4,
        out_specs=[VMEM] * 2,
        out_shape=[shaped((8, 3 * D), f32), shaped((8, D), f32)],
        compiler_params=params(4),
        cost_estimate=cost(1),
        name="finish",
    )(own, *got)


def per_device(latent, grad_latent, qkv_weight, out_weight, norm_gain, pair_bias):
    cols, rows, corner = strips(latent, grad_latent)
    cols = shift_grid(cols, 0, -1)
    rows = shift_grid(rows, -1, 0)
    corner = shift_grid(corner, -1, -1)
    gain = norm_gain.reshape(1, D)

    table = pair_bias.reshape(QUADS, 4, WIN, WIN).transpose(0, 3, 1, 2)
    upper = jnp.arange(WIN) % 72 // 12 >= 3
    differ = upper[:, None, None] != upper[None, None, :]
    bias = jnp.stack([table, jnp.where(differ, jnp.asarray(BLOCKED, bf16), table)])
    bias = bias.reshape(2, QUADS, WIN, LANES)
    pole = (lax.axis_index("lat") == lax.axis_size("lat") - 1).astype(jnp.int32).reshape(1)
    place = relative_rows()

    xw, gw, normed_t, normed = prologue(place, latent, grad_latent, cols, rows, corner, gain)
    att, gp, keep, send = some_quads(0, FIRST, pole, normed, normed_t, gw, qkv_weight, out_weight, bias)
    got = shift(send, "c", 1)
    att2, gp2, keep2, send2 = some_quads(FIRST, 1, pole, normed, normed_t, gw, qkv_weight, out_weight, bias)
    got2 = shift(send2, "c", 1)
    pieces = core_sum(keep, got)
    moved = ring(pieces, 0)
    att2, _ = lax.optimization_barrier((att2, pieces[1]))
    keep3, send3 = out_grads(place, att, att2, gw)
    got3 = shift(send3, "c", 1)
    pieces2 = core_sum(keep2, got2, keep3, got3)
    moved2 = ring(pieces2, 0)
    att2, _ = lax.optimization_barrier((att2, pieces2[1]))
    out_tile, grad_tile, cols, rows, corner = epilogue(
        att, att2, gp, gp2, out_weight, qkv_weight, xw, gw, gain
    )
    cols = shift_grid(cols, 0, 1)
    rows = shift_grid(rows, 1, 0)
    corner = shift_grid(corner, 1, 1)
    pieces = ring_sum(bf16, [pieces[0]] + moved, [pieces2[0]] + moved2)
    pieces = ring_sum(f32, [pieces[0]] + ring(pieces, 1))
    updated, grad_input = restored(out_tile, grad_tile, cols, rows, corner)
    qkv_grad, out_grad = finish(pieces[0], ring(pieces, 2))
    return (updated, grad_input, qkv_grad, out_grad)


def solution(mesh):
    in_specs = (P(None, "lat", "lon", None), P(None, "lat", "lon", None), P(), P(), P(), P())
    out_specs = (
        P(None, "lat", "lon", None),
        P(None, "lat", "lon", None),
        P(("lat", "lon"), None),
        P(("lat", "lon"), None),
    )
    return jax.shard_map(
        per_device, mesh=mesh, in_specs=in_specs, out_specs=out_specs, check_vma=False
    )
```

```python
import jax
import jax.numpy as jnp
from jax import lax
from jax.experimental import pallas as pl
from jax.experimental.pallas import tpu as pltpu
from jax.sharding import PartitionSpec as P

f32 = jnp.float32
bf16 = jnp.bfloat16
D = 1024
HEADS = 16
QUADS = 4
QW = 256
WIN = 144
TOK = 864
LANES = 4 * WIN
BLOCKED = -1e9
EPS = 1e-05


def nt(a, b):
    return lax.dot_general(a, b, (((1,), (1,)), ((), ())), preferred_element_type=f32)


def tn(a, b):
    return lax.dot_general(a, b, (((0,), (0,)), ((), ())), preferred_element_type=f32)


def nn(a, b):
    return jnp.dot(a, b, preferred_element_type=f32)


def index_of(x, y, z, c):
    return ((z % 2) * 4 + y) * 16 + (z // 2) * 8 + x * 2 + c


def place_of(index):
    lat, lon = index // 16, index % 16
    return dict(x=(lon // 2) % 4, y=lat % 4, z=(lon // 8) * 2 + lat // 4, c=lon % 2)


def my_place(axis):
    lat, lon = lax.axis_index("lat"), lax.axis_index("lon")
    return dict(x=(lon // 2) % 4, y=lat % 4, z=(lon // 8) * 2 + lat // 4, c=lon % 2)[axis]


def shift(value, axis, by):
    size = 2 if axis == "c" else 4
    pairs = []
    for src in range(128):
        place = place_of(src)
        place[axis] = (place[axis] + by) % size
        pairs.append((src, index_of(**place)))
    return lax.ppermute(value, ("lat", "lon"), pairs)


def shift_grid(value, dlat, dlon):
    pairs = []
    for lat in range(8):
        for lon in range(16):
            pairs.append((lat * 16 + lon, ((lat + dlat) % 8) * 16 + (lon + dlon) % 16))
    return lax.ppermute(value, ("lat", "lon"), pairs)


RINGS = ("xyz", "yxz")


def relative_rows():
    owner = place_of(jnp.arange(128, dtype=jnp.int32))
    off = {axis: (owner[axis] - my_place(axis)) % 4 for axis in "xyz"}
    along = [(off[a] * 4 + off[b]) * 4 + off[c] for a, b, c in RINGS]
    return (owner["c"] - my_place("c")) % 2 * 64 + jnp.where(owner["c"] == 0, along[0], along[1])


def ring_shift(value, stage, by):
    pairs = []
    for src in range(128):
        place = place_of(src)
        axis = RINGS[place["c"]][stage]
        place[axis] = (place[axis] + by) % 4
        pairs.append((src, index_of(**place)))
    return lax.ppermute(value, ("lat", "lon"), pairs)


def ring(pieces, stage):
    return [ring_shift(pieces[1], stage, 1), ring_shift(pieces[3], stage, -1), ring_shift(pieces[2], stage, 2)]


def params(mib):
    return pltpu.CompilerParams(vmem_limit_bytes=mib * 1024 * 1024)


def once(shape):
    return pl.BlockSpec(shape, lambda *_: (0,) * len(shape), pipeline_mode=pl.Buffered(1))


def cost(us):
    return pl.CostEstimate(flops=int(us * 1e9), bytes_accessed=int(us * 3e5), transcendentals=0)


def shaped(shape, dtype=bf16):
    return jax.ShapeDtypeStruct(shape, dtype)


VMEM = pl.BlockSpec(memory_space=pltpu.VMEM)
SMEM = pl.BlockSpec(memory_space=pltpu.SMEM)
COLS, ROWS, CORNER = 432, 288, 80


def strips_kernel(lat_ref, grad_ref, cols_ref, rows_ref, corner_ref, cs, rs, ks):
    ks[72:80] = jnp.zeros((8, D), f32)
    for which, tile in enumerate((lat_ref, grad_ref)):
        for l in range(2):
            for i in range(18):
                line = tile[l, i].astype(f32)
                at = (which * 2 + l) * 18 + i
                cs[at * 6 : at * 6 + 6] = line[:6]
                if i < 3:
                    at = (which * 2 + l) * 3 + i
                    rs[at * 24 : at * 24 + 24] = line
                    ks[at * 6 : at * 6 + 6] = line[:6]
    cols_ref[...] = cs[...].astype(bf16)
    rows_ref[...] = rs[...].astype(bf16)
    corner_ref[...] = ks[...].astype(bf16)


def strips(latent, grad_latent):
    return pl.pallas_call(
        strips_kernel,
        in_specs=[VMEM] * 2,
        out_specs=[VMEM] * 3,
        out_shape=[shaped((COLS, D)), shaped((ROWS, D)), shaped((CORNER, D))],
        scratch_shapes=[pltpu.VMEM((n, D), f32) for n in (COLS, ROWS, CORNER)],
        compiler_params=params(20),
        cost_estimate=cost(3),
        name="strips",
    )(latent, grad_latent)


def turned(value, place_ref, first, store):
    t = value.T
    for p in range(t.shape[0] // 8):
        store[pl.ds(pl.multiple_of(place_ref[first + p] * 8, 8), 8)] = t[8 * p : 8 * p + 8]


def prologue_kernel(
    place_ref, lat_ref, grad_ref, cols_ref, rows_ref, corner_ref, gain_ref, xw_ref, gw_ref, nt_ref, n_ref, xs, gs, ts, cs, ks
):
    cs[...] = cols_ref[...].astype(f32)
    ks[...] = corner_ref[...].astype(f32)
    for which, (tile, store) in enumerate(((lat_ref, xs), (grad_ref, gs))):
        for l in range(2):
            for i in range(18):
                if i < 15:
                    main = tile[l, i + 3].astype(f32)
                    at = ((which * 2 + l) * 18 + i + 3) * 6
                    side = cs[at : at + 6]
                else:
                    at = (which * 2 + l) * 3 + i - 15
                    main = rows_ref[at * 24 : at * 24 + 24].astype(f32)
                    side = ks[at * 6 : at * 6 + 6]
                left = (i // 6) * 2 * WIN + l * 72 + (i % 6) * 12
                right = left + WIN
                store[left : left + 12] = main[6:18]
                store[right : right + 6] = main[18:24]
                store[right + 6 : right + 12] = side
    gain = gain_ref[...]
    for w in range(6):
        rows = pl.ds(w * WIN, WIN)
        x = xs[rows]
        centred = x - jnp.mean(x, -1, keepdims=True)
        inv_std = lax.rsqrt(jnp.mean(centred * centred, -1, keepdims=True) + EPS)
        xw_ref[rows] = x.astype(bf16)
        gw_ref[rows] = gs[rows].astype(bf16)
        normed = centred * inv_std * gain
        n_ref[rows] = normed.astype(bf16)
        xs[rows] = normed
    for g in range(4):
        turned(xs[:, g * QW : (g + 1) * QW], place_ref, g * 32, ts)
    nt_ref[...] = ts[...].astype(bf16)


def prologue(place, latent, grad_latent, cols, rows, corner, gain):
    return pl.pallas_call(
        prologue_kernel,
        in_specs=[SMEM] + [VMEM] * 6,
        out_specs=[VMEM] * 4,
        out_shape=[shaped((TOK, D)), shaped((TOK, D)), shaped((D, TOK)), shaped((TOK, D))],
        scratch_shapes=[
            pltpu.VMEM((TOK, D), f32), pltpu.VMEM((TOK, D), f32), pltpu.VMEM((D, TOK), f32),
            pltpu.VMEM((COLS, D), f32), pltpu.VMEM((CORNER, D), f32),
        ],
        compiler_params=params(34),
        cost_estimate=cost(7),
        name="prologue",
    )(place, latent, grad_latent, cols, rows, corner, gain)


def attention(pole, n_ref, gw_ref, wq_ref, wk_ref, wv_ref, wo_ref, bias_ref, att_ref, gp_ref, q, k, v, da):
    n = n_ref[...]
    q[...] = nn(n, wq_ref[...]).astype(bf16)
    k[...] = nn(n, wk_ref[...]).astype(bf16)
    v[...] = nn(n, wv_ref[...]).astype(bf16)
    da[...] = nt(gw_ref[...], wo_ref[...]).astype(bf16)
    lane_head = lax.broadcasted_iota(jnp.int32, (WIN, QW), 1) // 64

    def apart(value):
        zero = jnp.zeros_like(value)
        return jnp.concatenate([jnp.where(lane_head == h, value, zero) for h in range(4)], 0)

    def gathered(stacked):
        out = stacked[:WIN]
        for h in range(1, 4):
            out = jnp.where(lane_head == h, stacked[h * WIN : (h + 1) * WIN], out)
        return out

    def window(w, carry):
        rows = pl.ds(pl.multiple_of(w * WIN, WIN), WIN)
        variant = jnp.where(w >= 4, pole, 0)
        qw, kw, vw, dw = q[rows], k[rows], v[rows], da[rows]
        q_apart = apart(qw * jnp.asarray(0.125, bf16))
        d_apart = apart(dw)
        s = nt(kw, q_apart) + bias_ref[variant, 0].astype(f32)
        dp = nt(vw, d_apart)
        e = jnp.exp(s - jnp.max(s, 0, keepdims=True))
        soft = e * (1.0 / jnp.sum(e, 0, keepdims=True))
        soft_b = soft.astype(bf16)
        inner = jnp.sum(soft * dp, 0, keepdims=True)
        ds = (soft * (dp - inner)).astype(bf16)
        att_ref[rows] = gathered(tn(soft_b, vw)).astype(bf16)
        gp_ref[2, rows] = nn(soft_b, d_apart).astype(bf16)
        gp_ref[1, rows] = nn(ds, q_apart).astype(bf16)
        gp_ref[0, rows] = (gathered(tn(ds, kw)) * 0.125).astype(bf16)
        return carry

    lax.fori_loop(0, 6, window, 0, unroll=2)


def split_rows(value, keep_ref, send_ref, at):
    keep_ref[:, at : at + QW] = value[:512].astype(bf16)
    send_ref[:, at : at + QW] = value[512:].astype(bf16)


def quads_kernel(
    pole_ref, n_ref, nt_ref, gw_ref, wq_ref, wk_ref, wv_ref, wo_ref, bias_ref,
    att_ref, gp_ref, keep_ref, send_ref, q, k, v, da,
):
    attention(pole_ref[0], n_ref, gw_ref, wq_ref, wk_ref, wv_ref, wo_ref, bias_ref, att_ref, gp_ref, q, k, v, da)
    for part in range(3):
        split_rows(nn(nt_ref[...], gp_ref[part]), keep_ref, send_ref, part * QW)


def out_grads_kernel(place_ref, before_ref, after_ref, gw_ref, keep_ref, send_ref, ts):
    for g in range(4):
        att = before_ref[:, g * QW : (g + 1) * QW] if g < 3 else after_ref[...]
        turned(att.astype(f32), place_ref, g * 32, ts)
    turned_att = ts[...].astype(bf16)
    for part in range(4):
        at = part * QW
        split_rows(nn(turned_att, gw_ref[:, at : at + QW]), keep_ref, send_ref, at)


FIRST = 3


def quad_specs(first):
    def columns(part):
        return pl.BlockSpec((D, QW), lambda g, *_: (0, part * QUADS + first + g))

    return [
        once((TOK, D)), once((D, TOK)), once((TOK, D)),
        columns(0), columns(1), columns(2),
        pl.BlockSpec((QW, D), lambda g, *_: (first + g, 0)),
        pl.BlockSpec((2, 1, WIN, LANES), lambda g, *_: (0, first + g, 0, 0)),
    ]


def some_quads(first, count, pole, normed, normed_t, gw, qkv_weight, out_weight, bias):
    return pl.pallas_call(
        quads_kernel,
        grid_spec=pltpu.PrefetchScalarGridSpec(
            num_scalar_prefetch=1,
            grid=(count,),
            in_specs=quad_specs(first),
            out_specs=[
                pl.BlockSpec((TOK, QW), lambda g, pole: (0, g)),
                pl.BlockSpec((3, TOK, QW), lambda g, pole: (0, 0, g)),
                pl.BlockSpec((512, 3 * QW), lambda g, pole: (0, g)),
                pl.BlockSpec((512, 3 * QW), lambda g, pole: (0, g)),
            ],
            scratch_shapes=[pltpu.VMEM((TOK, QW), bf16)] * 4,
        ),
        out_shape=[
            shaped((TOK, count * QW)), shaped((3, TOK, count * QW)),
            shaped((512, count * 3 * QW)), shaped((512, count * 3 * QW)),
        ],
        compiler_params=params(40),
        cost_estimate=cost(11 * count),
        name="quads",
    )(pole, normed, normed_t, gw, qkv_weight, qkv_weight, qkv_weight, out_weight, bias)


def out_grads(place, before, after, gw):
    return pl.pallas_call(
        out_grads_kernel,
        in_specs=[SMEM] + [VMEM] * 3,
        out_specs=[VMEM] * 2,
        out_shape=[shaped((512, D))] * 2,
        scratch_shapes=[pltpu.VMEM((D, TOK), f32)],
        compiler_params=params(20),
        cost_estimate=cost(7),
        name="out_grads",
    )(place, before, after, gw)


def epilogue_kernel(
    att_ref, att2_ref, gp_ref, gp2_ref, wo_ref, w_ref, xw_ref, gw_ref, gain_ref,
    out_ref, grad_ref, cols_ref, rows_ref, corner_ref, so, sg, cs, rs, ks,
):
    at_first = FIRST * QW
    x = xw_ref[...].astype(f32)
    so[...] = x + nn(att_ref[...], wo_ref[:at_first]) + nn(att2_ref[...], wo_ref[at_first:])
    gn = jnp.zeros((2 * WIN, D), f32)
    for part in range(3):
        gn = gn + nt(gp_ref[part], w_ref[:, part * D : part * D + at_first])
        gn = gn + nt(gp2_ref[part], w_ref[:, part * D + at_first : (part + 1) * D])
    centred = x - jnp.mean(x, -1, keepdims=True)
    inv_std = lax.rsqrt(jnp.mean(centred * centred, -1, keepdims=True) + EPS)
    unit = centred * inv_std
    e = gn * gain_ref[...]
    branch = inv_std * (e - jnp.mean(e, -1, keepdims=True) - unit * jnp.mean(e * unit, -1, keepdims=True))
    sg[...] = gw_ref[...].astype(f32) + branch
    step = pl.program_id(0)
    for which, (src, dst) in enumerate(((so, out_ref), (sg, grad_ref))):
        for l in range(2):
            for r in range(6):
                at = l * 72 + r * 12
                line = jnp.concatenate([src[at : at + 12], src[WIN + at : WIN + at + 12]], 0)
                dst[l, r] = line.astype(bf16)
                to = ((which * 2 + l) * 6 + r) * 6
                cs[to : to + 6] = line[18:]
                if r >= 3:
                    to = (which * 2 + l) * 3 + r - 3
                    rs[to * 24 : to * 24 + 24] = line
                    ks[to * 6 : to * 6 + 6] = line[18:]
    cols_ref[0] = cs[...].astype(bf16)

    @pl.when(step == 2)
    def _():
        ks[72:80] = jnp.zeros((8, D), f32)
        rows_ref[...] = rs[...].astype(bf16)
        corner_ref[...] = ks[...].astype(bf16)


def epilogue(att, att2, gp, gp2, out_weight, qkv_weight, xw, gw, gain):
    rows = 2 * WIN
    tile = pl.BlockSpec((2, 6, 24, D), lambda i: (0, i, 0, 0))
    return pl.pallas_call(
        epilogue_kernel,
        grid=(3,),
        in_specs=[
            pl.BlockSpec((rows, FIRST * QW), lambda i: (i, 0)),
            pl.BlockSpec((rows, QW), lambda i: (i, 0)),
            pl.BlockSpec((3, rows, FIRST * QW), lambda i: (0, i, 0)),
            pl.BlockSpec((3, rows, QW), lambda i: (0, i, 0)),
            once((D, D)),
            once((D, 3 * D)),
            pl.BlockSpec((rows, D), lambda i: (i, 0)),
            pl.BlockSpec((rows, D), lambda i: (i, 0)),
            pl.BlockSpec((1, D), lambda i: (0, 0)),
        ],
        out_specs=[
            tile, tile,
            pl.BlockSpec((1, WIN, D), lambda i: (i, 0, 0)),
            pl.BlockSpec((ROWS, D), lambda i: (0, 0)),
            pl.BlockSpec((CORNER, D), lambda i: (0, 0)),
        ],
        out_shape=[shaped((2, 18, 24, D))] * 2 + [shaped((3, WIN, D)), shaped((ROWS, D)), shaped((CORNER, D))],
        scratch_shapes=[pltpu.VMEM((n, D), f32) for n in (rows, rows, WIN, ROWS, CORNER)],
        compiler_params=params(40),
        cost_estimate=cost(16),
        name="epilogue",
    )(att, att2, gp, gp2, out_weight, qkv_weight, xw, gw, gain)


def restore_kernel(out_ref, grad_ref, cols_ref, rows_ref, corner_ref, updated_ref, back_ref, cs, ks):
    cs[...] = cols_ref[...].astype(f32)
    ks[...] = corner_ref[...].astype(f32)
    for which, (src, dst) in enumerate(((out_ref, updated_ref), (grad_ref, back_ref))):
        for l in range(2):
            for i in range(18):
                if i < 3:
                    at = (which * 2 + l) * 3 + i
                    main = rows_ref[at * 24 : at * 24 + 24].astype(f32)
                    side = ks[at * 6 : at * 6 + 6]
                else:
                    main = src[l, i - 3].astype(f32)
                    at = ((which * 2 + l) * 6 + (i - 3) % 6) * 6
                    side = cs[(i - 3) // 6, at : at + 6]
                dst[l, i] = jnp.concatenate([side, main[:18]], 0).astype(bf16)


def restored(out, grad, cols, rows, corner):
    return pl.pallas_call(
        restore_kernel,
        in_specs=[VMEM] * 5,
        out_specs=[VMEM] * 2,
        out_shape=[shaped((2, 18, 24, D))] * 2,
        scratch_shapes=[pltpu.VMEM((3, WIN, D), f32), pltpu.VMEM((CORNER, D), f32)],
        compiler_params=params(24),
        cost_estimate=cost(5),
        name="restore",
    )(out, grad, cols, rows, corner)


def core_sum_kernel(*refs):
    ins, outs = refs[:-4], refs[-4:]
    at = 0
    for keep, got in zip(ins[::2], ins[1::2]):
        columns = slice(at, at + keep.shape[1])
        for i, out in enumerate(outs):
            rows = slice(i * 128, i * 128 + 128)
            out[:, columns] = (keep[rows].astype(f32) + got[rows].astype(f32)).astype(bf16)
        at += keep.shape[1]


def core_sum(*pairs):
    columns = sum(v.shape[1] for v in pairs[::2])
    return pl.pallas_call(
        core_sum_kernel,
        in_specs=[VMEM] * len(pairs),
        out_specs=[VMEM] * 4,
        out_shape=[shaped((128, columns))] * 4,
        compiler_params=params(16),
        cost_estimate=cost(2),
        name="core_sum",
    )(*pairs)


def summed(refs):
    total = refs[0][...].astype(f32)
    for ref in refs[1:]:
        total = total + ref[...].astype(f32)
    return total


def ring_sum_kernel(*refs):
    ins, outs = refs[:-4], refs[-4:]
    at = 0
    for first in range(0, len(ins), 4):
        total = summed(ins[first : first + 4])
        rows = total.shape[0] // 4
        for i, out in enumerate(outs):
            out[:, at : at + total.shape[1]] = total[i * rows : (i + 1) * rows].astype(out.dtype)
        at += total.shape[1]


def ring_sum(dtype, *groups):
    rows = groups[0][0].shape[0] // 4
    columns = sum(group[0].shape[1] for group in groups)
    return pl.pallas_call(
        ring_sum_kernel,
        in_specs=[VMEM] * (4 * len(groups)),
        out_specs=[VMEM] * 4,
        out_shape=[shaped((rows, columns), dtype)] * 4,
        compiler_params=params(12),
        cost_estimate=cost(1),
        name="ring_sum",
    )(*[v for group in groups for v in group])


def finish_kernel(a, b, c, d, qkv_ref, out_ref):
    total = summed((a, b, c, d)) * (110592.0 ** (-0.5))
    for g in range(4):
        for part in range(3):
            at = (g * 3 + part) * QW
            to = part * D + g * QW
            qkv_ref[:, to : to + QW] = total[:, at : at + QW]
    out_ref[...] = total[:, 3 * D :]


def finish(own, got):
    return pl.pallas_call(
        finish_kernel,
        in_specs=[VMEM] * 4,
        out_specs=[VMEM] * 2,
        out_shape=[shaped((8, 3 * D), f32), shaped((8, D), f32)],
        compiler_params=params(4),
        cost_estimate=cost(1),
        name="finish",
    )(own, *got)


def per_device(latent, grad_latent, qkv_weight, out_weight, norm_gain, pair_bias):
    cols, rows, corner = strips(latent, grad_latent)
    cols = shift_grid(cols, 0, -1)
    rows = shift_grid(rows, -1, 0)
    corner = shift_grid(corner, -1, -1)
    gain = norm_gain.reshape(1, D)

    table = pair_bias.reshape(QUADS, 4, WIN, WIN).transpose(0, 3, 1, 2)
    upper = jnp.arange(WIN) % 72 // 12 >= 3
    differ = upper[:, None, None] != upper[None, None, :]
    bias = jnp.stack([table, jnp.where(differ, jnp.asarray(BLOCKED, bf16), table)])
    bias = bias.reshape(2, QUADS, WIN, LANES)
    pole = (lax.axis_index("lat") == lax.axis_size("lat") - 1).astype(jnp.int32).reshape(1)
    place = relative_rows()

    xw, gw, normed_t, normed = prologue(place, latent, grad_latent, cols, rows, corner, gain)
    att, gp, keep, send = some_quads(0, FIRST, pole, normed, normed_t, gw, qkv_weight, out_weight, bias)
    got = shift(send, "c", 1)
    att2, gp2, keep2, send2 = some_quads(FIRST, 1, pole, normed, normed_t, gw, qkv_weight, out_weight, bias)
    got2 = shift(send2, "c", 1)
    pieces = core_sum(keep, got)
    moved = ring(pieces, 0)
    att2, _ = lax.optimization_barrier((att2, pieces[1]))
    keep3, send3 = out_grads(place, att, att2, gw)
    got3 = shift(send3, "c", 1)
    pieces2 = core_sum(keep2, got2, keep3, got3)
    moved2 = ring(pieces2, 0)
    att2, _ = lax.optimization_barrier((att2, pieces2[1]))
    out_tile, grad_tile, cols, rows, corner = epilogue(
        att, att2, gp, gp2, out_weight, qkv_weight, xw, gw, gain
    )
    cols = shift_grid(cols, 0, 1)
    rows = shift_grid(rows, 1, 0)
    corner = shift_grid(corner, 1, 1)
    pieces = ring_sum(bf16, [pieces[0]] + moved, [pieces2[0]] + moved2)
    pieces = ring_sum(f32, [pieces[0]] + ring(pieces, 1))
    updated, grad_input = restored(out_tile, grad_tile, cols, rows, corner)
    qkv_grad, out_grad = finish(pieces[0], ring(pieces, 2))
    return (updated, grad_input, qkv_grad, out_grad)


def solution(mesh):
    in_specs = (P(None, "lat", "lon", None), P(None, "lat", "lon", None), P(), P(), P(), P())
    out_specs = (
        P(None, "lat", "lon", None),
        P(None, "lat", "lon", None),
        P(("lat", "lon"), None),
        P(("lat", "lon"), None),
    )
    return jax.shard_map(
        per_device, mesh=mesh, in_specs=in_specs, out_specs=out_specs, check_vma=False
    )
```

```python
import jax
import jax.numpy as jnp
from jax import lax
from jax.experimental import pallas as pl
from jax.experimental.pallas import tpu as pltpu
from jax.sharding import PartitionSpec as P

f32 = jnp.float32
bf16 = jnp.bfloat16
D = 1024
HEADS = 16
QUADS = 4
QW = 256
WIN = 144
TOK = 864
LANES = 4 * WIN
BLOCKED = -1e9
EPS = 1e-05


def nt(a, b):
    return lax.dot_general(a, b, (((1,), (1,)), ((), ())), preferred_element_type=f32)


def tn(a, b):
    return lax.dot_general(a, b, (((0,), (0,)), ((), ())), preferred_element_type=f32)


def nn(a, b):
    return jnp.dot(a, b, preferred_element_type=f32)


def index_of(x, y, z, c):
    return ((z % 2) * 4 + y) * 16 + (z // 2) * 8 + x * 2 + c


def place_of(index):
    lat, lon = index // 16, index % 16
    return dict(x=(lon // 2) % 4, y=lat % 4, z=(lon // 8) * 2 + lat // 4, c=lon % 2)


def my_place(axis):
    lat, lon = lax.axis_index("lat"), lax.axis_index("lon")
    return dict(x=(lon // 2) % 4, y=lat % 4, z=(lon // 8) * 2 + lat // 4, c=lon % 2)[axis]


def shift(value, axis, by):
    size = 2 if axis == "c" else 4
    pairs = []
    for src in range(128):
        place = place_of(src)
        place[axis] = (place[axis] + by) % size
        pairs.append((src, index_of(**place)))
    return lax.ppermute(value, ("lat", "lon"), pairs)


def shift_grid(value, dlat, dlon):
    pairs = []
    for lat in range(8):
        for lon in range(16):
            pairs.append((lat * 16 + lon, ((lat + dlat) % 8) * 16 + (lon + dlon) % 16))
    return lax.ppermute(value, ("lat", "lon"), pairs)


RINGS = ("xyz", "yxz")


def relative_rows():
    owner = place_of(jnp.arange(128, dtype=jnp.int32))
    off = {axis: (owner[axis] - my_place(axis)) % 4 for axis in "xyz"}
    along = [(off[a] * 4 + off[b]) * 4 + off[c] for a, b, c in RINGS]
    return (owner["c"] - my_place("c")) % 2 * 64 + jnp.where(owner["c"] == 0, along[0], along[1])


def ring_shift(value, stage, by):
    pairs = []
    for src in range(128):
        place = place_of(src)
        axis = RINGS[place["c"]][stage]
        place[axis] = (place[axis] + by) % 4
        pairs.append((src, index_of(**place)))
    return lax.ppermute(value, ("lat", "lon"), pairs)


def ring(pieces, stage):
    return [ring_shift(pieces[1], stage, 1), ring_shift(pieces[3], stage, -1), ring_shift(pieces[2], stage, 2)]


def params(mib):
    return pltpu.CompilerParams(vmem_limit_bytes=mib * 1024 * 1024)


def once(shape):
    return pl.BlockSpec(shape, lambda *_: (0,) * len(shape), pipeline_mode=pl.Buffered(1))


def cost(us):
    return pl.CostEstimate(flops=int(us * 1e9), bytes_accessed=int(us * 3e5), transcendentals=0)


def shaped(shape, dtype=bf16):
    return jax.ShapeDtypeStruct(shape, dtype)


VMEM = pl.BlockSpec(memory_space=pltpu.VMEM)
SMEM = pl.BlockSpec(memory_space=pltpu.SMEM)
COLS, ROWS, CORNER = 432, 288, 80


def strips_kernel(lat_ref, grad_ref, cols_ref, rows_ref, corner_ref, cs, rs, ks):
    ks[72:80] = jnp.zeros((8, D), f32)
    for which, tile in enumerate((lat_ref, grad_ref)):
        for l in range(2):
            for i in range(18):
                line = tile[l, i].astype(f32)
                at = (which * 2 + l) * 18 + i
                cs[at * 6 : at * 6 + 6] = line[:6]
                if i < 3:
                    at = (which * 2 + l) * 3 + i
                    rs[at * 24 : at * 24 + 24] = line
                    ks[at * 6 : at * 6 + 6] = line[:6]
    cols_ref[...] = cs[...].astype(bf16)
    rows_ref[...] = rs[...].astype(bf16)
    corner_ref[...] = ks[...].astype(bf16)


def strips(latent, grad_latent):
    return pl.pallas_call(
        strips_kernel,
        in_specs=[VMEM] * 2,
        out_specs=[VMEM] * 3,
        out_shape=[shaped((COLS, D)), shaped((ROWS, D)), shaped((CORNER, D))],
        scratch_shapes=[pltpu.VMEM((n, D), f32) for n in (COLS, ROWS, CORNER)],
        compiler_params=params(20),
        cost_estimate=cost(3),
        name="strips",
    )(latent, grad_latent)


def turned(value, place_ref, first, store):
    t = value.T
    for p in range(t.shape[0] // 8):
        store[pl.ds(pl.multiple_of(place_ref[first + p] * 8, 8), 8)] = t[8 * p : 8 * p + 8]


def prologue_kernel(
    place_ref, lat_ref, grad_ref, cols_ref, rows_ref, corner_ref, gain_ref, xw_ref, gw_ref, nt_ref, n_ref, xs, gs, ts, cs, ks
):
    cs[...] = cols_ref[...].astype(f32)
    ks[...] = corner_ref[...].astype(f32)
    for which, (tile, store) in enumerate(((lat_ref, xs), (grad_ref, gs))):
        for l in range(2):
            for i in range(18):
                if i < 15:
                    main = tile[l, i + 3].astype(f32)
                    at = ((which * 2 + l) * 18 + i + 3) * 6
                    side = cs[at : at + 6]
                else:
                    at = (which * 2 + l) * 3 + i - 15
                    main = rows_ref[at * 24 : at * 24 + 24].astype(f32)
                    side = ks[at * 6 : at * 6 + 6]
                left = (i // 6) * 2 * WIN + l * 72 + (i % 6) * 12
                right = left + WIN
                store[left : left + 12] = main[6:18]
                store[right : right + 6] = main[18:24]
                store[right + 6 : right + 12] = side
    gain = gain_ref[...]
    for w in range(6):
        rows = pl.ds(w * WIN, WIN)
        x = xs[rows]
        centred = x - jnp.mean(x, -1, keepdims=True)
        inv_std = lax.rsqrt(jnp.mean(centred * centred, -1, keepdims=True) + EPS)
        xw_ref[rows] = x.astype(bf16)
        gw_ref[rows] = gs[rows].astype(bf16)
        normed = centred * inv_std * gain
        n_ref[rows] = normed.astype(bf16)
        xs[rows] = normed
    for g in range(4):
        turned(xs[:, g * QW : (g + 1) * QW], place_ref, g * 32, ts)
    nt_ref[...] = ts[...].astype(bf16)


def prologue(place, latent, grad_latent, cols, rows, corner, gain):
    return pl.pallas_call(
        prologue_kernel,
        in_specs=[SMEM] + [VMEM] * 6,
        out_specs=[VMEM] * 4,
        out_shape=[shaped((TOK, D)), shaped((TOK, D)), shaped((D, TOK)), shaped((TOK, D))],
        scratch_shapes=[
            pltpu.VMEM((TOK, D), f32), pltpu.VMEM((TOK, D), f32), pltpu.VMEM((D, TOK), f32),
            pltpu.VMEM((COLS, D), f32), pltpu.VMEM((CORNER, D), f32),
        ],
        compiler_params=params(34),
        cost_estimate=cost(7),
        name="prologue",
    )(place, latent, grad_latent, cols, rows, corner, gain)


def attention(pole, n_ref, gw_ref, wq_ref, wk_ref, wv_ref, wo_ref, bias_ref, att_ref, gp_ref, q, k, v, da):
    n = n_ref[...]
    q[...] = nn(n, wq_ref[...]).astype(bf16)
    k[...] = nn(n, wk_ref[...]).astype(bf16)
    v[...] = nn(n, wv_ref[...]).astype(bf16)
    da[...] = nt(gw_ref[...], wo_ref[...]).astype(bf16)
    lane_head = lax.broadcasted_iota(jnp.int32, (WIN, QW), 1) // 64

    def apart(value):
        zero = jnp.zeros_like(value)
        return jnp.concatenate([jnp.where(lane_head == h, value, zero) for h in range(4)], 0)

    def gathered(stacked):
        out = stacked[:WIN]
        for h in range(1, 4):
            out = jnp.where(lane_head == h, stacked[h * WIN : (h + 1) * WIN], out)
        return out

    def window(w, carry):
        rows = pl.ds(pl.multiple_of(w * WIN, WIN), WIN)
        variant = jnp.where(w >= 4, pole, 0)
        qw, kw, vw, dw = q[rows], k[rows], v[rows], da[rows]
        q_apart = apart(qw * jnp.asarray(0.125, bf16))
        d_apart = apart(dw)
        s = nt(kw, q_apart) + bias_ref[variant, 0].astype(f32)
        dp = nt(vw, d_apart)
        e = jnp.exp(s - jnp.max(s, 0, keepdims=True))
        soft = e * (1.0 / jnp.sum(e, 0, keepdims=True))
        soft_b = soft.astype(bf16)
        inner = jnp.sum(soft * dp, 0, keepdims=True)
        ds = (soft * (dp - inner)).astype(bf16)
        att_ref[rows] = gathered(tn(soft_b, vw)).astype(bf16)
        gp_ref[2, rows] = nn(soft_b, d_apart).astype(bf16)
        gp_ref[1, rows] = nn(ds, q_apart).astype(bf16)
        gp_ref[0, rows] = (gathered(tn(ds, kw)) * 0.125).astype(bf16)
        return carry

    lax.fori_loop(0, 6, window, 0, unroll=2)


def split_rows(value, keep_ref, send_ref, at):
    keep_ref[:, at : at + QW] = value[:512].astype(bf16)
    send_ref[:, at : at + QW] = value[512:].astype(bf16)


def quads_kernel(
    pole_ref, n_ref, nt_ref, gw_ref, wq_ref, wk_ref, wv_ref, wo_ref, bias_ref,
    att_ref, gp_ref, keep_ref, send_ref, q, k, v, da,
):
    attention(pole_ref[0], n_ref, gw_ref, wq_ref, wk_ref, wv_ref, wo_ref, bias_ref, att_ref, gp_ref, q, k, v, da)
    for part in range(3):
        split_rows(nn(nt_ref[...], gp_ref[part]), keep_ref, send_ref, part * QW)


def out_grads_kernel(place_ref, before_ref, after_ref, gw_ref, keep_ref, send_ref, ts):
    for g in range(4):
        att = before_ref[:, g * QW : (g + 1) * QW] if g < 3 else after_ref[...]
        turned(att.astype(f32), place_ref, g * 32, ts)
    turned_att = ts[...].astype(bf16)
    for part in range(4):
        at = part * QW
        split_rows(nn(turned_att, gw_ref[:, at : at + QW]), keep_ref, send_ref, at)


FIRST = 3


def quad_specs(first):
    def columns(part):
        return pl.BlockSpec((D, QW), lambda g, *_: (0, part * QUADS + first + g))

    return [
        once((TOK, D)), once((D, TOK)), once((TOK, D)),
        columns(0), columns(1), columns(2),
        pl.BlockSpec((QW, D), lambda g, *_: (first + g, 0)),
        pl.BlockSpec((2, 1, WIN, LANES), lambda g, *_: (0, first + g, 0, 0)),
    ]


def some_quads(first, count, pole, normed, normed_t, gw, qkv_weight, out_weight, bias):
    return pl.pallas_call(
        quads_kernel,
        grid_spec=pltpu.PrefetchScalarGridSpec(
            num_scalar_prefetch=1,
            grid=(count,),
            in_specs=quad_specs(first),
            out_specs=[
                pl.BlockSpec((TOK, QW), lambda g, pole: (0, g)),
                pl.BlockSpec((3, TOK, QW), lambda g, pole: (0, 0, g)),
                pl.BlockSpec((512, 3 * QW), lambda g, pole: (0, g)),
                pl.BlockSpec((512, 3 * QW), lambda g, pole: (0, g)),
            ],
            scratch_shapes=[pltpu.VMEM((TOK, QW), bf16)] * 4,
        ),
        out_shape=[
            shaped((TOK, count * QW)), shaped((3, TOK, count * QW)),
            shaped((512, count * 3 * QW)), shaped((512, count * 3 * QW)),
        ],
        compiler_params=params(40),
        cost_estimate=cost(11 * count),
        name="quads",
    )(pole, normed, normed_t, gw, qkv_weight, qkv_weight, qkv_weight, out_weight, bias)


def out_grads(place, before, after, gw):
    return pl.pallas_call(
        out_grads_kernel,
        in_specs=[SMEM] + [VMEM] * 3,
        out_specs=[VMEM] * 2,
        out_shape=[shaped((512, D))] * 2,
        scratch_shapes=[pltpu.VMEM((D, TOK), f32)],
        compiler_params=params(20),
        cost_estimate=cost(7),
        name="out_grads",
    )(place, before, after, gw)


def epilogue_kernel(
    att_ref, att2_ref, gp_ref, gp2_ref, wo_ref, w_ref, xw_ref, gw_ref, gain_ref,
    out_ref, grad_ref, cols_ref, rows_ref, corner_ref, so, sg, cs, rs, ks,
):
    at_first = FIRST * QW
    x = xw_ref[...].astype(f32)
    so[...] = x + nn(att_ref[...], wo_ref[:at_first]) + nn(att2_ref[...], wo_ref[at_first:])
    gn = jnp.zeros((2 * WIN, D), f32)
    for part in range(3):
        gn = gn + nt(gp_ref[part], w_ref[:, part * D : part * D + at_first])
        gn = gn + nt(gp2_ref[part], w_ref[:, part * D + at_first : (part + 1) * D])
    centred = x - jnp.mean(x, -1, keepdims=True)
    inv_std = lax.rsqrt(jnp.mean(centred * centred, -1, keepdims=True) + EPS)
    unit = centred * inv_std
    e = gn * gain_ref[...]
    branch = inv_std * (e - jnp.mean(e, -1, keepdims=True) - unit * jnp.mean(e * unit, -1, keepdims=True))
    sg[...] = gw_ref[...].astype(f32) + branch
    step = pl.program_id(0)
    for which, (src, dst) in enumerate(((so, out_ref), (sg, grad_ref))):
        for l in range(2):
            for r in range(6):
                at = l * 72 + r * 12
                line = jnp.concatenate([src[at : at + 12], src[WIN + at : WIN + at + 12]], 0)
                dst[l, r] = line.astype(bf16)
                to = ((which * 2 + l) * 6 + r) * 6
                cs[to : to + 6] = line[18:]
                if r >= 3:
                    to = (which * 2 + l) * 3 + r - 3
                    rs[to * 24 : to * 24 + 24] = line
                    ks[to * 6 : to * 6 + 6] = line[18:]
    cols_ref[0] = cs[...].astype(bf16)

    @pl.when(step == 2)
    def _():
        ks[72:80] = jnp.zeros((8, D), f32)
        rows_ref[...] = rs[...].astype(bf16)
        corner_ref[...] = ks[...].astype(bf16)


def epilogue(att, att2, gp, gp2, out_weight, qkv_weight, xw, gw, gain):
    rows = 2 * WIN
    tile = pl.BlockSpec((2, 6, 24, D), lambda i: (0, i, 0, 0))
    return pl.pallas_call(
        epilogue_kernel,
        grid=(3,),
        in_specs=[
            pl.BlockSpec((rows, FIRST * QW), lambda i: (i, 0)),
            pl.BlockSpec((rows, QW), lambda i: (i, 0)),
            pl.BlockSpec((3, rows, FIRST * QW), lambda i: (0, i, 0)),
            pl.BlockSpec((3, rows, QW), lambda i: (0, i, 0)),
            once((D, D)),
            once((D, 3 * D)),
            pl.BlockSpec((rows, D), lambda i: (i, 0)),
            pl.BlockSpec((rows, D), lambda i: (i, 0)),
            pl.BlockSpec((1, D), lambda i: (0, 0)),
        ],
        out_specs=[
            tile, tile,
            pl.BlockSpec((1, WIN, D), lambda i: (i, 0, 0)),
            pl.BlockSpec((ROWS, D), lambda i: (0, 0)),
            pl.BlockSpec((CORNER, D), lambda i: (0, 0)),
        ],
        out_shape=[shaped((2, 18, 24, D))] * 2 + [shaped((3, WIN, D)), shaped((ROWS, D)), shaped((CORNER, D))],
        scratch_shapes=[pltpu.VMEM((n, D), f32) for n in (rows, rows, WIN, ROWS, CORNER)],
        compiler_params=params(40),
        cost_estimate=cost(16),
        name="epilogue",
    )(att, att2, gp, gp2, out_weight, qkv_weight, xw, gw, gain)


def restore_kernel(out_ref, grad_ref, cols_ref, rows_ref, corner_ref, updated_ref, back_ref, cs, ks):
    cs[...] = cols_ref[...].astype(f32)
    ks[...] = corner_ref[...].astype(f32)
    for which, (src, dst) in enumerate(((out_ref, updated_ref), (grad_ref, back_ref))):
        for l in range(2):
            for i in range(18):
                if i < 3:
                    at = (which * 2 + l) * 3 + i
                    main = rows_ref[at * 24 : at * 24 + 24].astype(f32)
                    side = ks[at * 6 : at * 6 + 6]
                else:
                    main = src[l, i - 3].astype(f32)
                    at = ((which * 2 + l) * 6 + (i - 3) % 6) * 6
                    side = cs[(i - 3) // 6, at : at + 6]
                dst[l, i] = jnp.concatenate([side, main[:18]], 0).astype(bf16)


def restored(out, grad, cols, rows, corner):
    return pl.pallas_call(
        restore_kernel,
        in_specs=[VMEM] * 5,
        out_specs=[VMEM] * 2,
        out_shape=[shaped((2, 18, 24, D))] * 2,
        scratch_shapes=[pltpu.VMEM((3, WIN, D), f32), pltpu.VMEM((CORNER, D), f32)],
        compiler_params=params(24),
        cost_estimate=cost(5),
        name="restore",
    )(out, grad, cols, rows, corner)


def core_sum_kernel(*refs):
    ins, outs = refs[:-4], refs[-4:]
    at = 0
    for keep, got in zip(ins[::2], ins[1::2]):
        columns = slice(at, at + keep.shape[1])
        for i, out in enumerate(outs):
            rows = slice(i * 128, i * 128 + 128)
            out[:, columns] = (keep[rows].astype(f32) + got[rows].astype(f32)).astype(bf16)
        at += keep.shape[1]


def core_sum(*pairs):
    columns = sum(v.shape[1] for v in pairs[::2])
    return pl.pallas_call(
        core_sum_kernel,
        in_specs=[VMEM] * len(pairs),
        out_specs=[VMEM] * 4,
        out_shape=[shaped((128, columns))] * 4,
        compiler_params=params(16),
        cost_estimate=cost(2),
        name="core_sum",
    )(*pairs)


def summed(refs):
    total = refs[0][...].astype(f32)
    for ref in refs[1:]:
        total = total + ref[...].astype(f32)
    return total


def ring_sum_kernel(*refs):
    ins, outs = refs[:-4], refs[-4:]
    at = 0
    for first in range(0, len(ins), 4):
        total = summed(ins[first : first + 4])
        rows = total.shape[0] // 4
        for i, out in enumerate(outs):
            out[:, at : at + total.shape[1]] = total[i * rows : (i + 1) * rows].astype(out.dtype)
        at += total.shape[1]


def ring_sum(dtype, *groups):
    rows = groups[0][0].shape[0] // 4
    columns = sum(group[0].shape[1] for group in groups)
    return pl.pallas_call(
        ring_sum_kernel,
        in_specs=[VMEM] * (4 * len(groups)),
        out_specs=[VMEM] * 4,
        out_shape=[shaped((rows, columns), dtype)] * 4,
        compiler_params=params(12),
        cost_estimate=cost(1),
        name="ring_sum",
    )(*[v for group in groups for v in group])


def finish_kernel(a, b, c, d, qkv_ref, out_ref):
    total = summed((a, b, c, d)) * (110592.0 ** (-0.5))
    for g in range(4):
        for part in range(3):
            at = (g * 3 + part) * QW
            to = part * D + g * QW
            qkv_ref[:, to : to + QW] = total[:, at : at + QW]
    out_ref[...] = total[:, 3 * D :]


def finish(own, got):
    return pl.pallas_call(
        finish_kernel,
        in_specs=[VMEM] * 4,
        out_specs=[VMEM] * 2,
        out_shape=[shaped((8, 3 * D), f32), shaped((8, D), f32)],
        compiler_params=params(4),
        cost_estimate=cost(1),
        name="finish",
    )(own, *got)


def per_device(latent, grad_latent, qkv_weight, out_weight, norm_gain, pair_bias):
    cols, rows, corner = strips(latent, grad_latent)
    cols = shift_grid(cols, 0, -1)
    rows = shift_grid(rows, -1, 0)
    corner = shift_grid(corner, -1, -1)
    gain = norm_gain.reshape(1, D)

    table = pair_bias.reshape(QUADS, 4, WIN, WIN).transpose(0, 3, 1, 2)
    upper = jnp.arange(WIN) % 72 // 12 >= 3
    differ = upper[:, None, None] != upper[None, None, :]
    bias = jnp.stack([table, jnp.where(differ, jnp.asarray(BLOCKED, bf16), table)])
    bias = bias.reshape(2, QUADS, WIN, LANES)
    pole = (lax.axis_index("lat") == lax.axis_size("lat") - 1).astype(jnp.int32).reshape(1)
    place = relative_rows()

    xw, gw, normed_t, normed = prologue(place, latent, grad_latent, cols, rows, corner, gain)
    att, gp, keep, send = some_quads(0, FIRST, pole, normed, normed_t, gw, qkv_weight, out_weight, bias)
    got = shift(send, "c", 1)
    att2, gp2, keep2, send2 = some_quads(FIRST, 1, pole, normed, normed_t, gw, qkv_weight, out_weight, bias)
    got2 = shift(send2, "c", 1)
    keep3, send3 = out_grads(place, att, att2, gw)
    got3 = shift(send3, "c", 1)
    pieces = core_sum(keep, got, keep2, got2, keep3, got3)
    moved = ring(pieces, 0)
    att2, _ = lax.optimization_barrier((att2, pieces[1]))
    out_tile, grad_tile, cols, rows, corner = epilogue(
        att, att2, gp, gp2, out_weight, qkv_weight, xw, gw, gain
    )
    cols = shift_grid(cols, 0, 1)
    rows = shift_grid(rows, 1, 0)
    corner = shift_grid(corner, 1, 1)
    pieces = ring_sum(bf16, [pieces[0]] + moved)
    pieces = ring_sum(f32, [pieces[0]] + ring(pieces, 1))
    updated, grad_input = restored(out_tile, grad_tile, cols, rows, corner)
    qkv_grad, out_grad = finish(pieces[0], ring(pieces, 2))
    return (updated, grad_input, qkv_grad, out_grad)


def solution(mesh):
    in_specs = (P(None, "lat", "lon", None), P(None, "lat", "lon", None), P(), P(), P(), P())
    out_specs = (
        P(None, "lat", "lon", None),
        P(None, "lat", "lon", None),
        P(("lat", "lon"), None),
        P(("lat", "lon"), None),
    )
    return jax.shard_map(
        per_device, mesh=mesh, in_specs=in_specs, out_specs=out_specs, check_vma=False
    )
```
